32 devices in a mesh: req: 8 (over z, x), sub: 4 (over y, core).
Axes of the slice: x: 2, y: 2, z: 4, core: 2. Of those that a mesh axis runs over, the one named last changes fastest.
Arguments:
- tokens: bfloat16 [4096, 2048], P(('req', 'sub')), may hold values from -6 to 6
- attn_gain: float32 [2048], replicated, may hold values from 0.25 to 1.75
- w_query: bfloat16 [2048, 1536], replicated, may hold values from -0.125 to 0.125
- w_latent: bfloat16 [2048, 576], replicated, may hold values from -0.125 to 0.125
- latent_gain: float32 [512], replicated, may hold values from 0.25 to 1.75
- w_key_up: bfloat16 [8, 128, 512], replicated, may hold values from -0.5 to 0.5
- w_value_up: bfloat16 [8, 512, 128], replicated, may hold values from -0.25 to 0.25
- w_out: bfloat16 [1024, 2048], replicated, may hold values from -0.1875 to 0.1875
- moe_gain: float32 [2048], replicated, may hold values from 0.25 to 1.75
- w_gate: bfloat16 [32, 2048, 704], P(('req', 'sub')), may hold values from -0.125 to 0.125
- w_up: bfloat16 [32, 2048, 704], P(('req', 'sub')), may hold values from -0.125 to 0.125
- w_down: bfloat16 [32, 704, 2048], P(('req', 'sub')), may hold values from -0.15625 to 0.15625
- expert_ids: int32 [4096, 6], P(('req', 'sub')), may hold values from 0 to 15, all different within a row; in each aligned block of 128 rows (0 to 127, 128 to 255, ...) at most 64 rows name the same one
- gate_weights: float32 [4096, 6], P(('req', 'sub')), may hold values from 0.1 to 0.6
- lengths: int32 [8, 3], P('req'), may hold values from 1 to 256, 512 in all within a row
- slab_group: int32 [8], P('req'), may hold values from 0 to 3
- owners: int32 [4], replicated, may hold values from 0 to 7, as said below
- prefix_pool: bfloat16 [8, 1024, 576], P('req'), as said below
Outputs:
- hidden_out: bfloat16 [4096, 2048], P(('req', 'sub'))
- new_cache: bfloat16 [4096, 576], P(('req', 'sub'))
The draws below stay inside these ranges and needn't reach their ends.
Inputs may be any that keep to these rules, and one draw needn't show every extreme that they name: `expert_ids`: each row names 6 different experts; in each aligned block of 128 rows (the rows of one device) no expert is named by more than 64 rows, and in some block one expert is named by exactly 64 rows. Each slab's 3 lengths sum to 512, and its longest request has exactly half of 512 tokens. 4 distinct slots, among them slot 0 and slot 7; group g's cached prefix is prefix_pool[owners[g]]. `prefix_pool`: each row holds 512 latent entries followed by 64 rotary key entries.
All inputs are finite; a program needn't handle non-finite values.
Results may differ from the reference program's by a relative error of at most 0.013.
The reference program's roundings to bfloat16 on the way count: a program that leaves them out, or rounds other values in their place, can miss the bound.
Values may be sent and summed in bfloat16 or wider, within the bound.
A program may use at most 128 MiB of HBM per device.

```python
import math
import jax
import jax.numpy as jnp
import numpy as np
from jax import lax

D = 2048
HEADS = 8
NOPE = 128
ROPE = 64
LAT = 512
VHEAD = 128
FFN = 1408
TOPK = 6
GROUPS = 4
PREFIX = 1024
REQ_SLAB = 3
TOK_DEV = 128
SLAB = 512
TOKENS = 4096
E = 16
CAP = 64
HALF = 704
N_REQ = 8


def draw_owners(key, part):
    pick_key = jax.random.fold_in(key, 21)
    order_key = jax.random.fold_in(key, 22)
    middle = jax.random.permutation(pick_key, N_REQ - 2)[:GROUPS - 2].astype(jnp.int32) + 1
    slots = jnp.concatenate([jnp.zeros((1,), jnp.int32), jnp.full((1,), N_REQ - 1, jnp.int32), middle])
    return jax.random.permutation(order_key, slots).astype(jnp.int32)


def draw_prefix_pool(key, part):
    base_key = jax.random.fold_in(key, 11)
    shape = (N_REQ, PREFIX, LAT + ROPE)
    values = jax.random.normal(base_key, shape, jnp.float32)
    return values.astype(jnp.bfloat16)


def touch_ends(entries, rng, smallest, high):
    index_at = [jax.random.randint(jax.random.fold_in(rng, axis), (), 0, length) for axis, length in enumerate(entries.shape)]
    widest = entries.shape.index(max(entries.shape))
    next_to = index_at[:widest] + [(index_at[widest] + 1) % entries.shape[widest]] + index_at[widest + 1:]
    return entries.at[tuple(index_at)].set(smallest).at[tuple(next_to)].set(high)


def block_scale(stream_key, dims, cuts, low, largest):
    factor_of = 1.0
    for position, parts in cuts:
        heights = jax.random.uniform(jax.random.fold_in(jax.random.fold_in(stream_key, 6), position), (parts,), jnp.float32, low / len(cuts), largest / len(cuts))
        factor_of = factor_of * jnp.repeat(jnp.exp(heights), dims[position] // parts).reshape((-1,) + (1,) * (len(dims) - 1 - position))
    return factor_of


def split_up(number_of, total, most, skew):
    loads = [(1 << 20) // math.isqrt(grade ** skew) + 1 for grade in range(2, number_of + 1)]
    rest, holding = total - most - (number_of - 1), [1] * (number_of - 1)
    while rest > 0:
        free = [i for i in range(number_of - 1) if holding[i] < most]
        pool, left = sum([loads[i] for i in free]), rest
        for i in free:
            addition = min(most - holding[i], max(1, left * loads[i] // pool), rest)
            holding[i] = holding[i] + addition
            rest = rest - addition
    return np.array([most] + holding)


def uneven(stream_key, number_of, total, limit, slope):
    if number_of == 2:
        one = jax.random.randint(stream_key, (), max(1, total - limit), min(limit, total - 1) + 1)
        return jnp.stack([one, total - one])
    tallies = jnp.asarray(split_up(number_of, total, limit, slope), jnp.int32)
    couples = (number_of - 1) // 2
    source_of, taker = tallies[1:1 + 2 * couples:2], tallies[2:2 + 2 * couples:2]
    margin = jnp.minimum(source_of - 1, limit - taker)
    passed = jax.random.randint(jax.random.fold_in(stream_key, 1), (couples,), 0, 1 << 20) % (margin + 1)
    tallies = tallies.at[1:1 + 2 * couples:2].set(source_of - passed).at[2:2 + 2 * couples:2].set(taker + passed)
    return tallies[jax.random.permutation(jax.random.fold_in(stream_key, 2), number_of)]


def shared_out(own_key, own, number, rows, count, top, most, slope):
    order = jax.random.permutation(own_key, count)
    packed, ordinary = portions_of(count, rows * top, most, slope, True), portions_of(count, rows * top, most, slope, False)
    places = jnp.arange(count)

    def named(sizes, offset_by):
        used = int((sizes > 0).sum())
        fixed = max(1, used // 4)
        moved = fixed + (places - fixed + offset_by * (used - fixed)) % max(1, count - fixed)
        return jnp.zeros((count,), jnp.int32).at[order[jnp.where(places < fixed, places, moved)]].set(jnp.asarray(sizes, jnp.int32))

    sizes = jnp.where(number % 4 == 0, named(packed, number // 4), named(ordinary, number - number // 4 - 1))
    mixed = jax.random.permutation(jax.random.fold_in(own, 3), count)
    donor, receiver = mixed[0:count // 2 * 2:2], mixed[1:count // 2 * 2:2]
    margin = jnp.minimum(sizes[donor] - 1, most - sizes[receiver]) // 2
    margin = jnp.where((donor == order[0]) | (receiver == order[0]) | (sizes[receiver] == 0), 0, jnp.maximum(margin, 0))
    moved = jax.random.randint(jax.random.fold_in(own, 4), (count // 2,), 0, 1 << 20) % (margin + 1)
    sizes = sizes.at[donor].add(-moved).at[receiver].add(moved)
    members = jnp.searchsorted(jnp.cumsum(sizes), jnp.arange(rows * top), side="right").astype(jnp.int32)
    table = members.reshape(top, rows).T
    table = table[jax.random.permutation(jax.random.fold_in(own, 1), rows)]
    offset_by = jax.random.randint(jax.random.fold_in(own, 2), (rows, 1), 0, top)
    return jnp.take_along_axis(table, (jnp.arange(top)[None, :] + offset_by) % top, axis=1)


def portions_of(count, total, most, skew, full):
    weights = [(1 << 20) // math.isqrt(rank ** skew) + 1 for rank in range(1, count + 1)]
    largest = most if full else min(most, max(-(-total // count), total * weights[0] // sum(weights)))
    least = 1 if total - largest >= count - 1 else 0
    holding, rest = [largest] + [least] * (count - 1), total - largest - least * (count - 1)
    while rest > 0:
        movable = [i for i in range(1, count) if holding[i] < largest] or [i for i in range(1, count) if holding[i] < most]
        whole, left = sum([weights[i] for i in movable]), rest
        for i in movable:
            more = min(most - holding[i], max(1, left * weights[i] // whole), rest)
            holding[i] = holding[i] + more
            rest = rest - more
    return np.array(holding)


def gaussian(stream_key, shape, deviation, most, pieces=(), kind=jnp.bfloat16):
    loudness = block_scale(stream_key, shape, pieces, -0.22, 0.18) if pieces else 1.0
    entries = jax.random.normal(stream_key, shape, jnp.float32) * deviation * loudness
    return jnp.minimum(jnp.maximum(entries, -most), most).astype(kind)


def setup_inputs(seed: int = 0) -> dict:
    keys = jax.random.split(jax.random.key(seed), 19)
    tokens = gaussian(keys[0], (TOKENS, D), 1.0, 6.0, ((0, 32),))
    attn_gain = jnp.clip(1.0 + 0.15 * jax.random.normal(keys[1], (D,), jnp.float32), 0.25, 1.75)
    w_query = gaussian(keys[2], (D, HEADS * (NOPE + ROPE)), D ** -0.5, 0.125)
    w_latent = gaussian(keys[3], (D, LAT + ROPE), D ** -0.5, 0.125)
    latent_gain = jnp.clip(1.0 + 0.15 * jax.random.normal(keys[4], (LAT,), jnp.float32), 0.25, 1.75)
    w_key_up = gaussian(keys[5], (HEADS, NOPE, LAT), NOPE ** -0.5, 0.5)
    w_value_up = gaussian(keys[6], (HEADS, LAT, VHEAD), LAT ** -0.5, 0.25)
    w_out = gaussian(keys[7], (HEADS * VHEAD, D), (HEADS * VHEAD) ** -0.5, 0.1875)
    moe_gain = jnp.clip(1.0 + 0.15 * jax.random.normal(keys[8], (D,), jnp.float32), 0.25, 1.75)
    w_gate = gaussian(keys[9], (2 * E, D, HALF), D ** -0.5, 0.125, ((0, 32),))
    w_up = gaussian(keys[10], (2 * E, D, HALF), D ** -0.5, 0.125, ((0, 32),))
    w_down = gaussian(keys[11], (2 * E, HALF, D), FFN ** -0.5, 0.15625, ((0, 32),))
    expert_ids_keys = jax.random.split(jax.random.fold_in(keys[12], 1), TOKENS // TOK_DEV)
    expert_ids_turns = jax.random.permutation(jax.random.fold_in(keys[12], 3), TOKENS // TOK_DEV)
    expert_ids = jax.vmap(lambda own, number: shared_out(jax.random.fold_in(keys[12], 2), own, number, TOK_DEV, E, TOPK, CAP, 2))(expert_ids_keys, expert_ids_turns).reshape((TOKENS, TOPK))
    gate_weights = jnp.clip(0.1 + 0.5 * jax.random.uniform(keys[13], (TOKENS, TOPK), jnp.float32) ** block_scale(keys[13], (TOKENS, TOPK), ((0, 32),), -0.2, 0.2), 0.1, 0.6)
    lengths = jax.vmap(lambda own: uneven(own, REQ_SLAB, SLAB, SLAB // 2, 2))(jax.random.split(keys[14], N_REQ)).reshape((N_REQ, REQ_SLAB)).astype(jnp.int32)
    slab_group = touch_ends(jax.random.randint(keys[15], (N_REQ,), 0, GROUPS), jax.random.fold_in(keys[15], 1), 0, GROUPS - 1).astype(jnp.int32)
    owners = draw_owners(jax.random.fold_in(keys[18], 71), 0)
    prefix_pool = draw_prefix_pool(jax.random.fold_in(keys[18], 71), 0)
    return dict(tokens=tokens, attn_gain=attn_gain, w_query=w_query, w_latent=w_latent, latent_gain=latent_gain, w_key_up=w_key_up, w_value_up=w_value_up, w_out=w_out, moe_gain=moe_gain, w_gate=w_gate, w_up=w_up, w_down=w_down, expert_ids=expert_ids, gate_weights=gate_weights, lengths=lengths, slab_group=slab_group, owners=owners, prefix_pool=prefix_pool)


EPSILON = 1e-06

def rms_scale(values, gain):
    return values * lax.rsqrt(lax.optimization_barrier(jnp.mean(values * values, axis=-1, keepdims=True)) + EPSILON) * gain

def angle_tables(positions, rope_width):
    half_width = rope_width // 2
    inverse = 10000.0 ** (-jnp.arange(half_width, dtype=jnp.float32) / half_width)
    angles = positions.astype(jnp.float32)[:, None] * inverse[None, :]
    return (jnp.cos(angles), jnp.sin(angles))

def rotate(values, cos_part, sin_part):
    half_width = values.shape[-1] // 2
    first_half = values[..., :half_width]
    second = values[..., half_width:]
    return jnp.concatenate([first_half * cos_part - second * sin_part, second * cos_part + first_half * sin_part], axis=-1)

def slab_layout(req_lengths, slab_rows):
    req_ends = jnp.cumsum(req_lengths).astype(jnp.int32)
    req_starts = req_ends - req_lengths
    slab_pos = jnp.arange(slab_rows, dtype=jnp.int32)
    segment = lax.optimization_barrier(jnp.sum((slab_pos[:, None] >= req_ends[None, :]).astype(jnp.int32), axis=1))
    member_of = segment[:, None] == jnp.arange(req_lengths.shape[0], dtype=jnp.int32)[None, :]
    seg_start = lax.optimization_barrier(jnp.sum(jnp.where(member_of, req_starts[None, :], 0), axis=1)).astype(jnp.int32)
    return (slab_pos, segment, slab_pos - seg_start)

def reference(tokens, attn_gain, w_query, w_latent, latent_gain, w_key_up, w_value_up, w_out, moe_gain, w_gate, w_up, w_down, expert_ids, gate_weights, lengths, slab_group, owners, prefix_pool):
    score_scale = (NOPE + ROPE) ** (-0.5)

    def attend_slab(inputs):
        slab_tokens, req_lengths, group_id = inputs
        slab_pos, segment, offset = slab_layout(req_lengths, SLAB)
        cos_part, sin_part = angle_tables(PREFIX + offset, ROPE)
        normed = rms_scale(slab_tokens.astype(jnp.float32), attn_gain).astype(jnp.bfloat16)
        latent = jnp.dot(normed, w_latent, preferred_element_type=jnp.float32)
        cache_rows = jnp.concatenate([rms_scale(latent[:, :LAT], latent_gain), rotate(latent[:, LAT:], cos_part, sin_part)], axis=1).astype(jnp.bfloat16)
        queries = jnp.dot(normed, w_query, preferred_element_type=jnp.float32).astype(jnp.bfloat16)
        queries = lax.optimization_barrier(queries).reshape(SLAB, HEADS, NOPE + ROPE).astype(jnp.float32)
        query_lat = jnp.einsum('thj,hjc->thc', queries[:, :, :NOPE], w_key_up.astype(jnp.float32))
        query_rot = rotate(queries[:, :, NOPE:], cos_part[:, None, :], sin_part[:, None, :])
        query_full = jnp.concatenate([query_lat, query_rot], axis=2).astype(jnp.bfloat16)
        key_rows = jnp.concatenate([prefix_pool[owners[group_id]], cache_rows], axis=0)
        query_full, key_rows = lax.optimization_barrier((query_full, key_rows))
        key_float = key_rows.astype(jnp.float32)
        scores = jnp.einsum('thc,kc->thk', query_full.astype(jnp.float32), key_float) * score_scale
        causal = (segment[None, :] == segment[:, None]) & (slab_pos[None, :] <= slab_pos[:, None])
        allowed = jnp.concatenate([jnp.ones((SLAB, PREFIX), dtype=bool), causal], axis=1)
        scores = jnp.where(allowed[:, None, :], scores, -jnp.inf)
        row_top = lax.optimization_barrier(jnp.max(scores, axis=2, keepdims=True))
        weights = jnp.exp(scores - row_top)
        denominator = lax.optimization_barrier(jnp.sum(weights, axis=2, keepdims=True))
        rounded = lax.optimization_barrier(weights.astype(jnp.bfloat16)).astype(jnp.float32)
        latent_out = (jnp.einsum('thk,kc->thc', rounded, key_float[:, :LAT]) / denominator).astype(jnp.bfloat16)
        latent_out = lax.optimization_barrier(latent_out).astype(jnp.float32)
        head_out = jnp.einsum('thc,hcv->thv', latent_out, w_value_up.astype(jnp.float32)).astype(jnp.bfloat16).reshape(SLAB, HEADS * VHEAD)
        residual = slab_tokens.astype(jnp.float32) + jnp.dot(head_out, w_out, preferred_element_type=jnp.float32)
        normed_mid = rms_scale(residual, moe_gain).astype(jnp.bfloat16)
        return (residual, normed_mid, cache_rows)
    residual, normed_mid, cache_rows = lax.map(attend_slab, (tokens.reshape(N_REQ, SLAB, D), lengths, slab_group))
    residual = residual.reshape(TOKENS, D)
    normed_mid = normed_mid.reshape(TOKENS, D)
    new_cache = cache_rows.reshape(TOKENS, LAT + ROPE)
    blocks = TOKENS // TOK_DEV
    flat_ids = expert_ids.reshape(blocks, TOK_DEV * TOPK)
    onehot = (flat_ids[:, :, None] == jnp.arange(E, dtype=jnp.int32)[None, None, :]).astype(jnp.int32)
    slot_index = lax.optimization_barrier(jnp.sum(onehot * (jnp.cumsum(onehot, axis=1) - 1), axis=2)).astype(jnp.int32)
    destination = (jnp.arange(blocks, dtype=jnp.int32)[:, None] * CAP + slot_index).reshape(TOKENS, TOPK)
    token_index = jnp.broadcast_to(jnp.arange(TOKENS, dtype=jnp.int32)[:, None], (TOKENS, TOPK)).reshape(-1)
    padded = jnp.concatenate([normed_mid, jnp.zeros((1, D), dtype=jnp.bfloat16)], axis=0)

    def expert_step(routed_sum, expert):
        slot_target = jnp.where(expert_ids == expert, destination, blocks * CAP).reshape(-1)
        slot_token = jnp.full((blocks * CAP,), TOKENS, dtype=jnp.int32).at[slot_target].set(token_index, mode='drop')
        slot_gate = jnp.zeros((blocks * CAP,), dtype=jnp.float32).at[slot_target].set(gate_weights.reshape(-1), mode='drop')
        slot_rows = padded[slot_token]
        gate_full = jnp.concatenate([w_gate[2 * expert], w_gate[2 * expert + 1]], axis=1)
        up_full = jnp.concatenate([w_up[2 * expert], w_up[2 * expert + 1]], axis=1)
        down_full = jnp.concatenate([w_down[2 * expert], w_down[2 * expert + 1]], axis=0)
        gate_proj = jnp.dot(slot_rows, gate_full, preferred_element_type=jnp.float32)
        up_proj = jnp.dot(slot_rows, up_full, preferred_element_type=jnp.float32)
        activated = (jax.nn.silu(gate_proj) * up_proj).astype(jnp.bfloat16)
        expert_out = jnp.dot(activated, down_full, preferred_element_type=jnp.float32).astype(jnp.bfloat16)
        expert_out = lax.optimization_barrier(expert_out).astype(jnp.float32)
        routed_sum = routed_sum.at[slot_token].add(slot_gate[:, None] * expert_out, mode='drop')
        return (routed_sum, None)
    routed_sum, unused = lax.scan(expert_step, jnp.zeros((TOKENS, D), dtype=jnp.float32), jnp.arange(E, dtype=jnp.int32))
    hidden_out = (residual + routed_sum).astype(jnp.bfloat16)
    return (hidden_out, new_cache)
```

```python
import jax
import jax.numpy as jnp
from jax import lax
from jax.sharding import PartitionSpec as P

EPSILON = 1e-06
FLOOR_SCORE = -1e30


def from_root(x, axis, root):
    mine = lax.axis_index(axis) == root
    return lax.psum(jnp.where(mine, x, jnp.zeros_like(x)), axis)


def rms_scale(values, gain):
    return values * lax.rsqrt(jnp.mean(values * values, axis=-1, keepdims=True) + EPSILON) * gain


def angle_tables(positions, rope_width):
    half_width = rope_width // 2
    inverse = 10000.0 ** (-jnp.arange(half_width, dtype=jnp.float32) / half_width)
    angles = positions.astype(jnp.float32)[:, None] * inverse[None, :]
    return (jnp.cos(angles), jnp.sin(angles))


def rotate(values, cos_part, sin_part):
    half_width = values.shape[-1] // 2
    first_half = values[..., :half_width]
    second = values[..., half_width:]
    return jnp.concatenate(
        [first_half * cos_part - second * sin_part, second * cos_part + first_half * sin_part],
        axis=-1,
    )


def slab_layout(req_lengths, slab_rows):
    req_count = req_lengths.shape[0]
    order = jnp.arange(req_count, dtype=jnp.int32)
    req_ends = jnp.sum(jnp.where(order[None, :] <= order[:, None], req_lengths[None, :], 0), axis=1)
    req_starts = req_ends - req_lengths
    slab_pos = jnp.arange(slab_rows, dtype=jnp.int32)
    segment = jnp.sum((slab_pos[:, None] >= req_ends[None, :]).astype(jnp.int32), axis=1)
    member_of = segment[:, None] == jnp.arange(req_lengths.shape[0], dtype=jnp.int32)[None, :]
    seg_start = jnp.sum(jnp.where(member_of, req_starts[None, :], 0), axis=1)
    return (slab_pos, segment, slab_pos - seg_start)


def block_attend(running, query_full, key_rows, allowed, score_scale, lat_width):
    row_top, denominator, weighted = running
    scores = (
        jnp.einsum("thc,kc->thk", query_full, key_rows, preferred_element_type=jnp.float32)
        * score_scale
    )
    scores = jnp.where(allowed[:, None, :], scores, FLOOR_SCORE)
    new_top = jnp.maximum(row_top, jnp.max(scores, axis=2))
    weights = jnp.where(allowed[:, None, :], jnp.exp(scores - new_top[:, :, None]), 0.0)
    rescale = jnp.exp(row_top - new_top)
    denominator = denominator * rescale + jnp.sum(weights, axis=2)
    weighted = weighted * rescale[:, :, None] + jnp.einsum(
        "thk,kc->thc",
        weights.astype(jnp.bfloat16),
        key_rows[:, :lat_width],
        preferred_element_type=jnp.float32,
    )
    return (new_top, denominator, weighted)


def route_tables(expert_ids, gate_weights, expert_count):
    experts = jnp.arange(expert_count, dtype=jnp.int32)
    named = expert_ids[:, :, None] == experts[None, None, :]
    chosen_of = jnp.sum(named.astype(jnp.float32), axis=1)
    gate_of = jnp.sum(jnp.where(named, gate_weights[:, :, None], 0.0), axis=1)
    return (chosen_of, gate_of)


def expert_half(slot_rows, gate_half, up_half, down_half):
    gate_proj = jnp.dot(slot_rows, gate_half, preferred_element_type=jnp.float32)
    up_proj = jnp.dot(slot_rows, up_half, preferred_element_type=jnp.float32)
    activated = (jax.nn.silu(gate_proj) * up_proj).astype(jnp.bfloat16)
    return jnp.dot(activated, down_half, preferred_element_type=jnp.float32)


def local(
    tokens,
    attn_gain,
    w_query,
    w_latent,
    latent_gain,
    w_key_up,
    w_value_up,
    w_out,
    moe_gain,
    w_gate,
    w_up,
    w_down,
    expert_ids,
    gate_weights,
    lengths,
    slab_group,
    owners,
    prefix_pool,
):
    rows_dev, model_width = tokens.shape
    head_count, nope_width, lat_width = w_key_up.shape
    rope_width = w_latent.shape[1] - lat_width
    prefix_len = prefix_pool.shape[1]
    sub_count = lax.axis_size("sub")
    device_count = lax.axis_size("req") * sub_count
    sub_index = lax.axis_index("sub")
    slab_rows = rows_dev * sub_count
    slab_pos, segment, offset = slab_layout(lengths[0], slab_rows)
    own_first = sub_index * rows_dev
    own_pos = lax.dynamic_slice_in_dim(slab_pos, own_first, rows_dev)
    own_seg = lax.dynamic_slice_in_dim(segment, own_first, rows_dev)
    own_offset = lax.dynamic_slice_in_dim(offset, own_first, rows_dev)
    cos_part, sin_part = angle_tables(prefix_len + own_offset, rope_width)
    normed = rms_scale(tokens.astype(jnp.float32), attn_gain).astype(jnp.bfloat16)
    latent = jnp.dot(normed, w_latent, preferred_element_type=jnp.float32)
    cache_rows = jnp.concatenate(
        [
            rms_scale(latent[:, :lat_width], latent_gain),
            rotate(latent[:, lat_width:], cos_part, sin_part),
        ],
        axis=1,
    ).astype(jnp.bfloat16)
    queries = jnp.dot(normed, w_query, preferred_element_type=jnp.float32).astype(jnp.bfloat16)
    queries = queries.reshape(rows_dev, head_count, nope_width + rope_width)
    query_lat = jnp.einsum(
        "thj,hjc->thc", queries[:, :, :nope_width], w_key_up, preferred_element_type=jnp.float32
    )
    query_rot = rotate(
        queries[:, :, nope_width:].astype(jnp.float32), cos_part[:, None, :], sin_part[:, None, :]
    )
    query_full = jnp.concatenate([query_lat, query_rot], axis=2).astype(jnp.bfloat16)
    score_scale = (nope_width + rope_width) ** (-0.5)
    my_group = slab_group[0]
    start_state = (
        jnp.full((rows_dev, head_count), FLOOR_SCORE, dtype=jnp.float32),
        jnp.zeros((rows_dev, head_count), dtype=jnp.float32),
        jnp.zeros((rows_dev, head_count, lat_width), dtype=jnp.float32),
    )
    local_prefix = prefix_pool[0]
    prefix = jnp.zeros_like(local_prefix)
    for member in range(owners.shape[0]):
        copied = from_root(local_prefix, "req", owners[member])
        prefix = jnp.where(my_group == member, copied, prefix)
    everyone = jnp.ones((rows_dev, prefix_len), dtype=bool)
    running = block_attend(start_state, query_full, prefix, everyone, score_scale, lat_width)
    key_block = lax.all_gather(cache_rows, "sub", axis=0, tiled=True)
    block_len = key_block.shape[0]
    key_pos = jnp.arange(block_len, dtype=jnp.int32)
    allowed = (segment[None, :] == own_seg[:, None]) & (key_pos[None, :] <= own_pos[:, None])
    running = block_attend(running, query_full, key_block, allowed, score_scale, lat_width)
    row_top, denominator, weighted = running
    latent_out = (weighted / denominator[:, :, None]).astype(jnp.bfloat16)
    head_out = jnp.einsum(
        "thc,hcv->thv", latent_out, w_value_up, preferred_element_type=jnp.float32
    ).astype(jnp.bfloat16)
    head_out = head_out.reshape(rows_dev, head_count * w_value_up.shape[2])
    residual = tokens.astype(jnp.float32) + jnp.dot(
        head_out, w_out, preferred_element_type=jnp.float32
    )
    normed_mid = rms_scale(residual, moe_gain).astype(jnp.bfloat16)
    top_count = expert_ids.shape[1]
    expert_count = device_count // 2
    capacity = 4 * rows_dev * top_count // (3 * expert_count)
    chosen_of, gate_of = route_tables(expert_ids, gate_weights, expert_count)
    row_order = jnp.arange(rows_dev, dtype=jnp.int32)
    earlier = (row_order[None, :] < row_order[:, None]).astype(jnp.bfloat16)
    slot_of = jnp.dot(earlier, chosen_of.astype(jnp.bfloat16), preferred_element_type=jnp.float32)
    slots = jnp.arange(capacity, dtype=jnp.float32)
    at_slot = (slot_of[:, :, None] == slots[None, None, :]) & (chosen_of[:, :, None] > 0.0)
    placing = at_slot.astype(jnp.bfloat16).reshape(rows_dev, expert_count * capacity)
    mixing = jnp.where(at_slot, gate_of[:, :, None], 0.0).reshape(rows_dev, expert_count * capacity)
    outbound = jnp.einsum(
        "ts,td->sd", placing, normed_mid, preferred_element_type=jnp.float32
    ).astype(jnp.bfloat16)
    doubled = jnp.broadcast_to(
        outbound.reshape(expert_count, 1, capacity, model_width),
        (expert_count, 2, capacity, model_width),
    )
    arrived = lax.all_to_all(
        doubled.reshape(device_count, capacity, model_width),
        ("req", "sub"),
        split_axis=0,
        concat_axis=0,
        tiled=True,
    )
    partial_value = expert_half(arrived.reshape(-1, model_width), w_gate[0], w_up[0], w_down[0])
    returned = lax.all_to_all(
        partial_value.reshape(device_count, capacity, model_width).astype(jnp.bfloat16),
        ("req", "sub"),
        split_axis=0,
        concat_axis=0,
        tiled=True,
    ).astype(jnp.float32)
    merged = returned.reshape(expert_count, 2, capacity, model_width)
    expert_out = (merged[:, 0] + merged[:, 1]).astype(jnp.bfloat16)
    expert_flat = expert_out.reshape(-1, model_width)
    mixing_high = mixing.astype(jnp.bfloat16)
    mixing_low = (mixing - mixing_high.astype(jnp.float32)).astype(jnp.bfloat16)
    routed_sum = jnp.dot(mixing_high, expert_flat, preferred_element_type=jnp.float32) + jnp.dot(
        mixing_low, expert_flat, preferred_element_type=jnp.float32
    )
    hidden_out = (residual + routed_sum).astype(jnp.bfloat16)
    return (hidden_out, cache_rows)


def solution(mesh):
    in_specs = (
        P(("req", "sub"), None),
        P(),
        P(),
        P(),
        P(),
        P(),
        P(),
        P(),
        P(),
        P(("req", "sub"), None, None),
        P(("req", "sub"), None, None),
        P(("req", "sub"), None, None),
        P(("req", "sub"), None),
        P(("req", "sub"), None),
        P("req", None),
        P("req"),
        P(),
        P("req", None, None),
    )
    out_specs = (P(("req", "sub"), None), P(("req", "sub"), None))
    return jax.shard_map(local, mesh=mesh, in_specs=in_specs, out_specs=out_specs, check_vma=False)
```

```python
import jax
import jax.numpy as jnp
from jax import lax
from jax.sharding import PartitionSpec as P

EPSILON = 1e-06
FLOOR_SCORE = -1e30


def swap_cores(x):
    pairs = [(i, i + 1 - 2 * (i % 2)) for i in range(lax.axis_size("sub"))]
    return lax.ppermute(x, "sub", pairs)


def group_prefix(prefix_pool, owner):
    sub_count = lax.axis_size("sub")
    share = prefix_pool.shape[1] // sub_count
    mine = lax.dynamic_slice_in_dim(prefix_pool[0], lax.axis_index("sub") * share, share)
    every = lax.all_gather(mine, "req", axis=0)
    picked = lax.dynamic_index_in_dim(every, owner, 0, keepdims=False)
    return lax.all_gather(picked, "sub", axis=0, tiled=True)


def rms_scale(values, gain):
    return values * lax.rsqrt(jnp.mean(values * values, axis=-1, keepdims=True) + EPSILON) * gain


def angle_tables(positions, rope_width):
    half_width = rope_width // 2
    inverse = 10000.0 ** (-jnp.arange(half_width, dtype=jnp.float32) / half_width)
    angles = positions.astype(jnp.float32)[:, None] * inverse[None, :]
    return (jnp.cos(angles), jnp.sin(angles))


def rotate(values, cos_part, sin_part):
    half_width = values.shape[-1] // 2
    first_half = values[..., :half_width]
    second = values[..., half_width:]
    return jnp.concatenate(
        [first_half * cos_part - second * sin_part, second * cos_part + first_half * sin_part],
        axis=-1,
    )


def slab_layout(req_lengths, slab_rows):
    req_count = req_lengths.shape[0]
    order = jnp.arange(req_count, dtype=jnp.int32)
    req_ends = jnp.sum(jnp.where(order[None, :] <= order[:, None], req_lengths[None, :], 0), axis=1)
    req_starts = req_ends - req_lengths
    slab_pos = jnp.arange(slab_rows, dtype=jnp.int32)
    segment = jnp.sum((slab_pos[:, None] >= req_ends[None, :]).astype(jnp.int32), axis=1)
    member_of = segment[:, None] == jnp.arange(req_lengths.shape[0], dtype=jnp.int32)[None, :]
    seg_start = jnp.sum(jnp.where(member_of, req_starts[None, :], 0), axis=1)
    return (slab_pos, segment, slab_pos - seg_start)


def block_attend(running, query_full, key_rows, allowed, score_scale, lat_width):
    row_top, denominator, weighted = running
    scores = (
        jnp.einsum("thc,kc->thk", query_full, key_rows, preferred_element_type=jnp.float32)
        * score_scale
    )
    scores = jnp.where(allowed[:, None, :], scores, FLOOR_SCORE)
    new_top = jnp.maximum(row_top, jnp.max(scores, axis=2))
    weights = jnp.where(allowed[:, None, :], jnp.exp(scores - new_top[:, :, None]), 0.0)
    rescale = jnp.exp(row_top - new_top)
    denominator = denominator * rescale + jnp.sum(weights, axis=2)
    weighted = weighted * rescale[:, :, None] + jnp.einsum(
        "thk,kc->thc",
        weights.astype(jnp.bfloat16),
        key_rows[:, :lat_width],
        preferred_element_type=jnp.float32,
    )
    return (new_top, denominator, weighted)


def route_tables(expert_ids, gate_weights, expert_count):
    experts = jnp.arange(expert_count, dtype=jnp.int32)
    named = expert_ids[:, :, None] == experts[None, None, :]
    chosen_of = jnp.sum(named.astype(jnp.float32), axis=1)
    gate_of = jnp.sum(jnp.where(named, gate_weights[:, :, None], 0.0), axis=1)
    return (chosen_of, gate_of)


def hidden_half(slot_rows, gate_half, up_half):
    gate_proj = jnp.dot(slot_rows, gate_half, preferred_element_type=jnp.float32)
    up_proj = jnp.dot(slot_rows, up_half, preferred_element_type=jnp.float32)
    return (jax.nn.silu(gate_proj) * up_proj).astype(jnp.bfloat16)


def local(
    tokens,
    attn_gain,
    w_query,
    w_latent,
    latent_gain,
    w_key_up,
    w_value_up,
    w_out,
    moe_gain,
    w_gate,
    w_up,
    w_down,
    expert_ids,
    gate_weights,
    lengths,
    slab_group,
    owners,
    prefix_pool,
):
    rows_dev, model_width = tokens.shape
    head_count, nope_width, lat_width = w_key_up.shape
    rope_width = w_latent.shape[1] - lat_width
    prefix_len = prefix_pool.shape[1]
    sub_count = lax.axis_size("sub")
    device_count = lax.axis_size("req") * sub_count
    sub_index = lax.axis_index("sub")
    slab_rows = rows_dev * sub_count
    gate_other = swap_cores(w_gate[0])
    up_other = swap_cores(w_up[0])
    down_other = swap_cores(w_down[0])
    slab_pos, segment, offset = slab_layout(lengths[0], slab_rows)
    own_first = sub_index * rows_dev
    own_pos = lax.dynamic_slice_in_dim(slab_pos, own_first, rows_dev)
    own_seg = lax.dynamic_slice_in_dim(segment, own_first, rows_dev)
    own_offset = lax.dynamic_slice_in_dim(offset, own_first, rows_dev)
    cos_part, sin_part = angle_tables(prefix_len + own_offset, rope_width)
    normed = rms_scale(tokens.astype(jnp.float32), attn_gain).astype(jnp.bfloat16)
    latent = jnp.dot(normed, w_latent, preferred_element_type=jnp.float32)
    cache_rows = jnp.concatenate(
        [
            rms_scale(latent[:, :lat_width], latent_gain),
            rotate(latent[:, lat_width:], cos_part, sin_part),
        ],
        axis=1,
    ).astype(jnp.bfloat16)
    queries = jnp.dot(normed, w_query, preferred_element_type=jnp.float32).astype(jnp.bfloat16)
    queries = queries.reshape(rows_dev, head_count, nope_width + rope_width)
    query_lat = jnp.einsum(
        "thj,hjc->thc", queries[:, :, :nope_width], w_key_up, preferred_element_type=jnp.float32
    )
    query_rot = rotate(
        queries[:, :, nope_width:].astype(jnp.float32), cos_part[:, None, :], sin_part[:, None, :]
    )
    query_full = jnp.concatenate([query_lat, query_rot], axis=2).astype(jnp.bfloat16)
    score_scale = (nope_width + rope_width) ** (-0.5)
    my_group = slab_group[0]
    start_state = (
        jnp.full((rows_dev, head_count), FLOOR_SCORE, dtype=jnp.float32),
        jnp.zeros((rows_dev, head_count), dtype=jnp.float32),
        jnp.zeros((rows_dev, head_count, lat_width), dtype=jnp.float32),
    )
    prefix = group_prefix(prefix_pool, owners[my_group])
    everyone = jnp.ones((rows_dev, prefix_len), dtype=bool)
    running = block_attend(start_state, query_full, prefix, everyone, score_scale, lat_width)
    key_block = lax.all_gather(cache_rows, "sub", axis=0, tiled=True)
    block_len = key_block.shape[0]
    key_pos = jnp.arange(block_len, dtype=jnp.int32)
    allowed = (segment[None, :] == own_seg[:, None]) & (key_pos[None, :] <= own_pos[:, None])
    running = block_attend(running, query_full, key_block, allowed, score_scale, lat_width)
    row_top, denominator, weighted = running
    latent_out = (weighted / denominator[:, :, None]).astype(jnp.bfloat16)
    head_out = jnp.einsum(
        "thc,hcv->thv", latent_out, w_value_up, preferred_element_type=jnp.float32
    ).astype(jnp.bfloat16)
    head_out = head_out.reshape(rows_dev, head_count * w_value_up.shape[2])
    residual = tokens.astype(jnp.float32) + jnp.dot(
        head_out, w_out, preferred_element_type=jnp.float32
    )
    normed_mid = rms_scale(residual, moe_gain).astype(jnp.bfloat16)
    top_count = expert_ids.shape[1]
    expert_count = device_count // 2
    capacity = 4 * rows_dev * top_count // (3 * expert_count)
    chosen_of, gate_of = route_tables(expert_ids, gate_weights, expert_count)
    row_order = jnp.arange(rows_dev, dtype=jnp.int32)
    earlier = (row_order[None, :] < row_order[:, None]).astype(jnp.bfloat16)
    slot_of = jnp.dot(earlier, chosen_of.astype(jnp.bfloat16), preferred_element_type=jnp.float32)
    slots = jnp.arange(capacity, dtype=jnp.float32)
    at_slot = (slot_of[:, :, None] == slots[None, None, :]) & (chosen_of[:, :, None] > 0.0)
    placing = at_slot.astype(jnp.bfloat16).reshape(rows_dev, expert_count * capacity)
    mixing = jnp.where(at_slot, gate_of[:, :, None], 0.0).reshape(rows_dev, expert_count * capacity)
    outbound = jnp.einsum(
        "ts,td->sd", placing, normed_mid, preferred_element_type=jnp.float32
    ).astype(jnp.bfloat16)
    core_groups = [list(range(core, device_count, 2)) for core in range(2)]
    arrived = lax.all_to_all(
        outbound.reshape(expert_count, capacity, model_width),
        ("req", "sub"),
        split_axis=0,
        concat_axis=0,
        axis_index_groups=core_groups,
        tiled=True,
    ).reshape(-1, model_width)
    expert_rows = jnp.dot(
        hidden_half(arrived, w_gate[0], w_up[0]), w_down[0], preferred_element_type=jnp.float32
    ) + jnp.dot(
        hidden_half(arrived, gate_other, up_other), down_other, preferred_element_type=jnp.float32
    )
    expert_out = lax.all_to_all(
        expert_rows.astype(jnp.bfloat16).reshape(expert_count, capacity, model_width),
        ("req", "sub"),
        split_axis=0,
        concat_axis=0,
        axis_index_groups=core_groups,
        tiled=True,
    )
    expert_flat = expert_out.reshape(-1, model_width)
    mixing_high = mixing.astype(jnp.bfloat16)
    mixing_low = (mixing - mixing_high.astype(jnp.float32)).astype(jnp.bfloat16)
    routed_sum = jnp.dot(mixing_high, expert_flat, preferred_element_type=jnp.float32) + jnp.dot(
        mixing_low, expert_flat, preferred_element_type=jnp.float32
    )
    hidden_out = (residual + routed_sum).astype(jnp.bfloat16)
    return (hidden_out, cache_rows)


def solution(mesh):
    in_specs = (
        P(("req", "sub"), None),
        P(),
        P(),
        P(),
        P(),
        P(),
        P(),
        P(),
        P(),
        P(("req", "sub"), None, None),
        P(("req", "sub"), None, None),
        P(("req", "sub"), None, None),
        P(("req", "sub"), None),
        P(("req", "sub"), None),
        P("req", None),
        P("req"),
        P(),
        P("req", None, None),
    )
    out_specs = (P(("req", "sub"), None), P(("req", "sub"), None))
    return jax.shard_map(local, mesh=mesh, in_specs=in_specs, out_specs=out_specs, check_vma=False)
```

```python
import functools

import jax
import jax.numpy as jnp
from jax import lax
from jax.experimental import pallas as pl
from jax.experimental.pallas import tpu as pltpu
from jax.sharding import PartitionSpec as P

EPSILON = 1e-06
FLOOR_SCORE = -1e30


def swap_cores(x):
    pairs = [(i, i + 1 - 2 * (i % 2)) for i in range(lax.axis_size("sub"))]
    return lax.ppermute(x, "sub", pairs)


def group_prefix(prefix_pool, owner):
    sub_count = lax.axis_size("sub")
    share = prefix_pool.shape[1] // sub_count
    mine = lax.dynamic_slice_in_dim(prefix_pool[0], lax.axis_index("sub") * share, share)
    every = lax.all_gather(mine, "req", axis=0)
    picked = lax.dynamic_index_in_dim(every, owner, 0, keepdims=False)
    return lax.all_gather(picked, "sub", axis=0, tiled=True)


def rms_scale(values, gain):
    return values * lax.rsqrt(jnp.mean(values * values, axis=-1, keepdims=True) + EPSILON) * gain


def angle_tables(positions, rope_width):
    half_width = rope_width // 2
    inverse = 10000.0 ** (-jnp.arange(half_width, dtype=jnp.float32) / half_width)
    angles = positions.astype(jnp.float32)[:, None] * inverse[None, :]
    return (jnp.cos(angles), jnp.sin(angles))


def rotate(values, cos_part, sin_part):
    half_width = values.shape[-1] // 2
    first_half = values[..., :half_width]
    second = values[..., half_width:]
    return jnp.concatenate(
        [first_half * cos_part - second * sin_part, second * cos_part + first_half * sin_part],
        axis=-1,
    )


def slab_layout(req_lengths, slab_rows):
    req_count = req_lengths.shape[0]
    order = jnp.arange(req_count, dtype=jnp.int32)
    req_ends = jnp.sum(jnp.where(order[None, :] <= order[:, None], req_lengths[None, :], 0), axis=1)
    req_starts = req_ends - req_lengths
    slab_pos = jnp.arange(slab_rows, dtype=jnp.int32)
    segment = jnp.sum((slab_pos[:, None] >= req_ends[None, :]).astype(jnp.int32), axis=1)
    member_of = segment[:, None] == jnp.arange(req_lengths.shape[0], dtype=jnp.int32)[None, :]
    seg_start = jnp.sum(jnp.where(member_of, req_starts[None, :], 0), axis=1)
    return (slab_pos, segment, slab_pos - seg_start)


def block_attend(running, query_full, key_rows, allowed, score_scale, lat_width):
    row_top, denominator, weighted = running
    scores = (
        jnp.einsum("thc,kc->thk", query_full, key_rows, preferred_element_type=jnp.float32)
        * score_scale
    )
    scores = jnp.where(allowed[:, None, :], scores, FLOOR_SCORE)
    new_top = jnp.maximum(row_top, jnp.max(scores, axis=2))
    weights = jnp.where(allowed[:, None, :], jnp.exp(scores - new_top[:, :, None]), 0.0)
    rescale = jnp.exp(row_top - new_top)
    denominator = denominator * rescale + jnp.sum(weights, axis=2)
    weighted = weighted * rescale[:, :, None] + jnp.einsum(
        "thk,kc->thc",
        weights.astype(jnp.bfloat16),
        key_rows[:, :lat_width],
        preferred_element_type=jnp.float32,
    )
    return (new_top, denominator, weighted)


PLANE = 4
VMEM_BYTES = 40 * 1024 * 1024


def place_of():
    req = lax.axis_index("req")
    sub = lax.axis_index("sub")
    return (req // 2, req % 2, sub // 2, sub % 2)


def line_device(step, line_count):
    z, x, y, core = place_of()
    return (((z + step + line_count) % line_count) * 2 + x, y * 2 + core)


def mate_place(mate, x, y):
    return (x + (mate // 2) * (1 - 2 * x), y + (mate % 2) * (1 - 2 * y))


def plane_device(mate):
    z, x, y, core = place_of()
    other_x, other_y = mate_place(mate, x, y)
    return (z * 2 + other_x, other_y * 2 + core)


def remote(src, dst, send_sem, recv_sem, device):
    return pltpu.make_async_remote_copy(
        src_ref=src,
        dst_ref=dst,
        send_sem=send_sem,
        recv_sem=recv_sem,
        device_id=device,
        device_id_type=pl.DeviceIdType.MESH,
    )


def greet(line_count):
    barrier = pltpu.get_barrier_semaphore()
    partners = [line_device(step, line_count) for step in range(1, line_count)]
    partners += [plane_device(mate) for mate in range(1, PLANE)]
    for partner in partners:
        pl.semaphore_signal(
            barrier, inc=1, device_id=partner, device_id_type=pl.DeviceIdType.MESH
        )
    pl.semaphore_wait(barrier, len(partners))


def dispatch_kernel(
    line_count, rows_ref, place_ref, out_ref, held, packed,
    line_send, line_recv, plane_send, plane_recv, own_sem,
):
    greet(line_count)
    along = {}
    for step in range(1, line_count):
        along[step] = remote(
            rows_ref, held.at[step], line_send.at[step], line_recv.at[step],
            line_device(step, line_count),
        )
        along[step].start()
    started = []
    for step in range(line_count):
        if step:
            along[step].wait_recv()
        source = rows_ref[...] if step == 0 else held[step]
        for mate in (3, 1, 2, 0):
            packed[step, mate] = jnp.dot(
                place_ref[step, mate], source, preferred_element_type=jnp.float32
            ).astype(jnp.bfloat16)
            if mate:
                copy = remote(
                    packed.at[step, mate], out_ref.at[step, mate],
                    plane_send.at[step, mate], plane_recv.at[step, mate], plane_device(mate),
                )
            else:
                copy = pltpu.make_async_copy(
                    packed.at[step, 0], out_ref.at[step, 0], own_sem.at[step]
                )
            copy.start()
            started.append(copy)
    for step in range(1, line_count):
        along[step].wait_send()
    for copy in started:
        copy.wait()


def dispatch(rows, place):
    line_count, _, capacity, row_count = place.shape
    width = rows.shape[1]
    return pl.pallas_call(
        functools.partial(dispatch_kernel, line_count),
        out_shape=jax.ShapeDtypeStruct((line_count, PLANE, capacity, width), jnp.bfloat16),
        in_specs=[pl.BlockSpec(memory_space=pltpu.VMEM)] * 2,
        out_specs=pl.BlockSpec(memory_space=pl.ANY),
        scratch_shapes=[
            pltpu.VMEM((line_count, row_count, width), jnp.bfloat16),
            pltpu.VMEM((line_count, PLANE, capacity, width), jnp.bfloat16),
            pltpu.SemaphoreType.DMA((line_count,)),
            pltpu.SemaphoreType.DMA((line_count,)),
            pltpu.SemaphoreType.DMA((line_count, PLANE)),
            pltpu.SemaphoreType.DMA((line_count, PLANE)),
            pltpu.SemaphoreType.DMA((line_count,)),
        ],
        compiler_params=pltpu.CompilerParams(
            collective_id=0, has_side_effects=True, vmem_limit_bytes=VMEM_BYTES
        ),
    )(rows, place)


def combine_kernel(
    line_count, rows_ref, high_ref, low_ref, residual_ref, out_ref, back, leaving, landed, total,
    plane_send, plane_recv, own_sem, line_send, line_recv,
):
    greet(line_count)
    order = list(range(1, line_count)) + [0]
    across = {}
    for step in order:
        for mate in (3, 1, 2, 0):
            if mate:
                copy = remote(
                    rows_ref.at[step, mate], back.at[step, mate],
                    plane_send.at[step, mate], plane_recv.at[step, mate], plane_device(mate),
                )
            else:
                copy = pltpu.make_async_copy(
                    rows_ref.at[step, 0], back.at[step, 0], own_sem.at[step]
                )
            copy.start()
            across[step, mate] = copy
    home = {}
    for step in order:
        for mate in range(PLANE):
            across[step, mate].wait()
        _, _, capacity, width = back.shape
        expert_rows = back[step].reshape(PLANE * capacity, width)
        mixed = jnp.dot(
            high_ref[step], expert_rows, preferred_element_type=jnp.float32
        ) + jnp.dot(low_ref[step], expert_rows, preferred_element_type=jnp.float32)
        if step:
            leaving[step] = mixed.astype(jnp.bfloat16)
            home[step] = remote(
                leaving.at[step], landed.at[step], line_send.at[step], line_recv.at[step],
                line_device(-step, line_count),
            )
            home[step].start()
        else:
            total[...] = residual_ref[...] + mixed
    for step in range(1, line_count):
        home[step].wait()
        total[...] += landed[step].astype(jnp.float32)
    out_ref[...] = total[...].astype(jnp.bfloat16)


def combine(expert_rows, mixing_high, mixing_low, residual):
    line_count, _, capacity, width = expert_rows.shape
    row_count = residual.shape[0]
    vmem = pl.BlockSpec(memory_space=pltpu.VMEM)
    return pl.pallas_call(
        functools.partial(combine_kernel, line_count),
        out_shape=jax.ShapeDtypeStruct((row_count, width), jnp.bfloat16),
        in_specs=[pl.BlockSpec(memory_space=pl.ANY), vmem, vmem, vmem],
        out_specs=vmem,
        scratch_shapes=[
            pltpu.VMEM((line_count, PLANE, capacity, width), jnp.bfloat16),
            pltpu.VMEM((line_count, row_count, width), jnp.bfloat16),
            pltpu.VMEM((line_count, row_count, width), jnp.bfloat16),
            pltpu.VMEM((row_count, width), jnp.float32),
            pltpu.SemaphoreType.DMA((line_count, PLANE)),
            pltpu.SemaphoreType.DMA((line_count, PLANE)),
            pltpu.SemaphoreType.DMA((line_count,)),
            pltpu.SemaphoreType.DMA((line_count,)),
            pltpu.SemaphoreType.DMA((line_count,)),
        ],
        compiler_params=pltpu.CompilerParams(
            collective_id=1, has_side_effects=True, vmem_limit_bytes=VMEM_BYTES
        ),
    )(expert_rows, mixing_high, mixing_low, residual)


def route_tables(expert_ids, gate_weights, capacity):
    row_count, top_count = expert_ids.shape
    line_count = lax.axis_size("req") // 2
    z, x, y, _ = place_of()
    both = jnp.concatenate([expert_ids.astype(jnp.float32), gate_weights], axis=1).T
    every = lax.all_gather(both, "req", axis=0)
    line = jnp.stack(
        [
            lax.dynamic_index_in_dim(
                every, ((z - step + line_count) % line_count) * 2 + x, 0, keepdims=False
            )
            for step in range(line_count)
        ]
    )
    experts = []
    for mate in range(PLANE):
        other_x, other_y = mate_place(mate, x, y)
        experts.append(z * PLANE + other_x * 2 + other_y)
    experts = jnp.stack(experts).astype(jnp.float32)
    named = line[:, None, :top_count, :] == experts[None, :, None, None]
    chosen = jnp.sum(named.astype(jnp.float32), axis=2)
    gates = jnp.sum(jnp.where(named, line[:, None, top_count:, :], 0.0), axis=2)
    row_order = jnp.arange(row_count, dtype=jnp.int32)
    earlier = (row_order[:, None] < row_order[None, :]).astype(jnp.bfloat16)
    slot_of = jnp.einsum(
        "lmu,ut->lmt", chosen.astype(jnp.bfloat16), earlier, preferred_element_type=jnp.float32
    )
    slots = jnp.arange(capacity, dtype=jnp.float32)
    at_slot = (slot_of[:, :, None, :] == slots[None, None, :, None]) & (chosen[:, :, None, :] > 0.0)
    place = at_slot.astype(jnp.bfloat16)
    mixing = jnp.where(at_slot, gates[:, :, None, :], 0.0)
    mixing = mixing.reshape(line_count, PLANE * capacity, row_count).transpose(0, 2, 1)
    mixing_high = mixing.astype(jnp.bfloat16)
    mixing_low = (mixing - mixing_high.astype(jnp.float32)).astype(jnp.bfloat16)
    return (place, mixing_high, mixing_low)


def hidden_half(slot_rows, gate_half, up_half):
    gate_proj = jnp.dot(slot_rows, gate_half, preferred_element_type=jnp.float32)
    up_proj = jnp.dot(slot_rows, up_half, preferred_element_type=jnp.float32)
    return (jax.nn.silu(gate_proj) * up_proj).astype(jnp.bfloat16)


def local(
    tokens,
    attn_gain,
    w_query,
    w_latent,
    latent_gain,
    w_key_up,
    w_value_up,
    w_out,
    moe_gain,
    w_gate,
    w_up,
    w_down,
    expert_ids,
    gate_weights,
    lengths,
    slab_group,
    owners,
    prefix_pool,
):
    rows_dev, model_width = tokens.shape
    head_count, nope_width, lat_width = w_key_up.shape
    rope_width = w_latent.shape[1] - lat_width
    prefix_len = prefix_pool.shape[1]
    sub_count = lax.axis_size("sub")
    device_count = lax.axis_size("req") * sub_count
    sub_index = lax.axis_index("sub")
    slab_rows = rows_dev * sub_count
    top_count = expert_ids.shape[1]
    expert_count = device_count // 2
    capacity = 4 * rows_dev * top_count // (3 * expert_count)
    place, mixing_high, mixing_low = route_tables(expert_ids, gate_weights, capacity)
    gate_other = swap_cores(w_gate[0])
    up_other = swap_cores(w_up[0])
    down_other = swap_cores(w_down[0])
    slab_pos, segment, offset = slab_layout(lengths[0], slab_rows)
    own_first = sub_index * rows_dev
    own_pos = lax.dynamic_slice_in_dim(slab_pos, own_first, rows_dev)
    own_seg = lax.dynamic_slice_in_dim(segment, own_first, rows_dev)
    own_offset = lax.dynamic_slice_in_dim(offset, own_first, rows_dev)
    cos_part, sin_part = angle_tables(prefix_len + own_offset, rope_width)
    normed = rms_scale(tokens.astype(jnp.float32), attn_gain).astype(jnp.bfloat16)
    latent = jnp.dot(normed, w_latent, preferred_element_type=jnp.float32)
    cache_rows = jnp.concatenate(
        [
            rms_scale(latent[:, :lat_width], latent_gain),
            rotate(latent[:, lat_width:], cos_part, sin_part),
        ],
        axis=1,
    ).astype(jnp.bfloat16)
    queries = jnp.dot(normed, w_query, preferred_element_type=jnp.float32).astype(jnp.bfloat16)
    queries = queries.reshape(rows_dev, head_count, nope_width + rope_width)
    query_lat = jnp.einsum(
        "thj,hjc->thc", queries[:, :, :nope_width], w_key_up, preferred_element_type=jnp.float32
    )
    query_rot = rotate(
        queries[:, :, nope_width:].astype(jnp.float32), cos_part[:, None, :], sin_part[:, None, :]
    )
    query_full = jnp.concatenate([query_lat, query_rot], axis=2).astype(jnp.bfloat16)
    score_scale = (nope_width + rope_width) ** (-0.5)
    my_group = slab_group[0]
    start_state = (
        jnp.full((rows_dev, head_count), FLOOR_SCORE, dtype=jnp.float32),
        jnp.zeros((rows_dev, head_count), dtype=jnp.float32),
        jnp.zeros((rows_dev, head_count, lat_width), dtype=jnp.float32),
    )
    prefix = group_prefix(prefix_pool, owners[my_group])
    everyone = jnp.ones((rows_dev, prefix_len), dtype=bool)
    running = block_attend(start_state, query_full, prefix, everyone, score_scale, lat_width)
    key_block = lax.all_gather(cache_rows, "sub", axis=0, tiled=True)
    block_len = key_block.shape[0]
    key_pos = jnp.arange(block_len, dtype=jnp.int32)
    allowed = (segment[None, :] == own_seg[:, None]) & (key_pos[None, :] <= own_pos[:, None])
    running = block_attend(running, query_full, key_block, allowed, score_scale, lat_width)
    row_top, denominator, weighted = running
    latent_out = (weighted / denominator[:, :, None]).astype(jnp.bfloat16)
    head_out = jnp.einsum(
        "thc,hcv->thv", latent_out, w_value_up, preferred_element_type=jnp.float32
    ).astype(jnp.bfloat16)
    head_out = head_out.reshape(rows_dev, head_count * w_value_up.shape[2])
    residual = tokens.astype(jnp.float32) + jnp.dot(
        head_out, w_out, preferred_element_type=jnp.float32
    )
    normed_mid = rms_scale(residual, moe_gain).astype(jnp.bfloat16)
    arrived = dispatch(normed_mid, place).reshape(-1, model_width)
    expert_rows = jnp.dot(
        hidden_half(arrived, w_gate[0], w_up[0]), w_down[0], preferred_element_type=jnp.float32
    ) + jnp.dot(
        hidden_half(arrived, gate_other, up_other), down_other, preferred_element_type=jnp.float32
    )
    expert_out = expert_rows.astype(jnp.bfloat16).reshape(-1, PLANE, capacity, model_width)
    hidden_out = combine(expert_out, mixing_high, mixing_low, residual)
    return (hidden_out, cache_rows)


def solution(mesh):
    in_specs = (
        P(("req", "sub"), None),
        P(),
        P(),
        P(),
        P(),
        P(),
        P(),
        P(),
        P(),
        P(("req", "sub"), None, None),
        P(("req", "sub"), None, None),
        P(("req", "sub"), None, None),
        P(("req", "sub"), None),
        P(("req", "sub"), None),
        P("req", None),
        P("req"),
        P(),
        P("req", None, None),
    )
    out_specs = (P(("req", "sub"), None), P(("req", "sub"), None))
    return jax.shard_map(local, mesh=mesh, in_specs=in_specs, out_specs=out_specs, check_vma=False)
```
